256 devices in a mesh: hst: 16 (over z, y_lo), seq: 16 (over x, y_hi, core).
Axes of the slice: x: 4, y: 4 (y_hi: 2, y_lo: 2; y = y_hi * 2 + y_lo), z: 8, core: 2. Of those that a mesh axis runs over, the one named last changes fastest.
Arguments:
- queries: bfloat16 [16, 16, 2048, 128], P('hst', 'seq'), may hold values from -9 to 9
- keys: bfloat16 [16, 16, 2048, 128], P('hst', 'seq'), may hold values from -9 to 9
- values: bfloat16 [16, 16, 2048, 128], P('hst', 'seq'), may hold values from -6 to 6
- cotangent: bfloat16 [16, 2048, 3072], P('hst', 'seq'), may hold values from -6 to 6
- gate: float32 [16, 3072], P('hst'), may hold values from -4 to 4
- w_out: bfloat16 [2048, 3072], P('seq'), may hold values from -0.125 to 0.125
Outputs:
- grad_queries: bfloat16 [16, 16, 2048, 128], P('hst', 'seq')
- grad_keys: bfloat16 [16, 16, 2048, 128], P('hst', 'seq')
- grad_values: bfloat16 [16, 16, 2048, 128], P('hst', 'seq')
- grad_out_proj: float32 [2048, 3072], P('seq')
The draws below stay inside these ranges and needn't reach their ends.
All inputs are finite; a program needn't handle non-finite values.
Results may differ from the reference program's by a relative error of at most 0.025.
Values may be sent and summed in bfloat16 or wider, within the bound.
No kernel may reach another device: no remote copies, remote signals or barrier semaphores. Data moves between devices by JAX's collectives and lax.ppermute only.
A program may use at most 128 MiB of HBM per device.

```python
import jax
import jax.numpy as jnp
from jax import lax

D = 3072
DH = 128
TOK_DEV = 128
HEADS = 16
SEQ = 2048
CLIPS = 16
HD = 2048
N_SEQ = 16


def drawn_pair(key, mix):
    key_query, key_key, key_qrow, key_krow = jax.random.split(key, 4)
    shape = (CLIPS, HEADS, SEQ, DH)
    queries = jnp.clip(jax.random.normal(key_query, shape, jnp.float32), -5.0, 5.0)
    keys = jnp.clip(jax.random.normal(key_key, shape, jnp.float32), -5.0, 5.0)
    pairs = 4
    span_query = SEQ // pairs
    span_key = SEQ // (2 * pairs)
    offsets = jnp.arange(pairs, dtype=jnp.int32)
    query_rows = offsets * span_query + jax.random.randint(key_qrow, (CLIPS, HEADS, pairs), 0, span_query)
    key_rows = offsets * span_key + jax.random.randint(key_krow, (CLIPS, HEADS, pairs), 0, span_key)
    second_rows = key_rows + SEQ // 2
    positions = jnp.arange(SEQ, dtype=jnp.int32)
    pick_query = (positions[None, None, None, :] == query_rows[..., None]).astype(jnp.float32)
    pick_key = (positions[None, None, None, :] == key_rows[..., None]).astype(jnp.float32)
    pick_second = (positions[None, None, None, :] == second_rows[..., None]).astype(jnp.float32)
    mask_query = jnp.sum(pick_query, axis=2)[..., None]
    mask_key = (jnp.sum(pick_key, axis=2) + jnp.sum(pick_second, axis=2))[..., None]
    queries = queries * (1.0 - mix * mask_query)
    keys = keys * (1.0 - mix * mask_key)
    return (queries, keys)


def draw_queries(key, part):
    mix = 0.0
    return drawn_pair(key, mix)[0].astype(jnp.bfloat16)


def draw_keys(key, part):
    mix = 0.0
    return drawn_pair(key, mix)[1].astype(jnp.bfloat16)


def block_scale(stream_key, shape, cuts, low, high):
    level = 1.0
    for dim, parts in cuts:
        steps = jax.random.uniform(jax.random.fold_in(jax.random.fold_in(stream_key, 6), dim), (parts,), jnp.float32, low / len(cuts), high / len(cuts))
        level = level * jnp.repeat(jnp.exp(steps), shape[dim] // parts).reshape((-1,) + (1,) * (len(shape) - 1 - dim))
    return level


def normal_values(own_key, extent, scale, limit, shards=(), kind=jnp.bfloat16):
    gain = block_scale(own_key, extent, shards, -0.22, 0.18) if shards else 1.0
    array = jax.random.normal(own_key, extent, jnp.float32) * scale * gain
    return jnp.minimum(jnp.maximum(array, -limit), limit).astype(kind)


def setup_inputs(seed: int = 0) -> dict:
    key_of = jax.random.split(jax.random.key(seed), 7)
    return {
        "queries": draw_queries(jax.random.fold_in(key_of[6], 71), 0),
        "keys": draw_keys(jax.random.fold_in(key_of[6], 71), 0),
        "values": normal_values(key_of[2], (CLIPS, HEADS, SEQ, DH), 1.0, 6.0, ((0, 16), (1, 16))),
        "cotangent": normal_values(key_of[3], (CLIPS, SEQ, D), 1.0, 6.0, ((0, 16), (1, 16))),
        "gate": normal_values(key_of[4], (CLIPS, D), 1.0, 4.0, ((0, 16),), jnp.float32),
        "w_out": normal_values(key_of[5], (HD, D), HD ** -0.5, 0.125, ((0, 16),)),
    }


def contract_last(left, right):
    return lax.dot_general(left, right, (((1,), (1,)), ((), ())), preferred_element_type=jnp.float32)


def contract_first(left, right):
    return lax.dot_general(left, right, (((0,), (0,)), ((), ())), preferred_element_type=jnp.float32)


def head_probs(query_rows, key_rows, scale):
    scores = contract_last(query_rows, key_rows) * scale
    row_max = jnp.max(scores, axis=-1, keepdims=True)
    log_total = row_max + jnp.log(jnp.sum(jnp.exp(scores - row_max), axis=-1, keepdims=True))
    return jnp.exp(scores - log_total)


def reference(queries, keys, values, cotangent, gate, w_out):
    scale = 1.0 / (DH ** 0.5)
    flat_q = queries.reshape(CLIPS * HEADS, SEQ, DH)
    flat_k = keys.reshape(CLIPS * HEADS, SEQ, DH)
    flat_v = values.reshape(CLIPS * HEADS, SEQ, DH)

    def forward(items):
        query_head, key_head, value_head = items
        probs = head_probs(query_head, key_head, scale)
        return jnp.dot(probs.astype(jnp.bfloat16), value_head, preferred_element_type=jnp.float32).astype(jnp.bfloat16)

    attn = lax.map(forward, (flat_q, flat_k, flat_v)).reshape(CLIPS, HEADS, SEQ, DH)
    attn_tokens = attn.transpose(0, 2, 1, 3).reshape(CLIPS, SEQ, HEADS * DH)
    grad_proj = (cotangent.astype(jnp.float32) * gate[:, None, :]).astype(jnp.bfloat16)

    block_count = CLIPS * N_SEQ
    attn_blocks = attn_tokens.reshape(block_count, TOK_DEV, HEADS * DH)
    proj_blocks = grad_proj.reshape(block_count, TOK_DEV, D)

    def accumulate(total, items):
        attn_part, proj_part = items
        rounded = contract_first(attn_part, proj_part).astype(jnp.bfloat16)
        rounded = lax.optimization_barrier(rounded)
        return total + rounded.astype(jnp.float32), None

    grad_out_proj, _ = lax.scan(accumulate, jnp.zeros((HEADS * DH, D), jnp.float32), (attn_blocks, proj_blocks))

    grad_attn = contract_last(grad_proj.reshape(CLIPS * SEQ, D), w_out).astype(jnp.bfloat16)
    grad_attn = grad_attn.reshape(CLIPS, SEQ, HEADS, DH).transpose(0, 2, 1, 3).reshape(CLIPS * HEADS, SEQ, DH)

    def backward(items):
        query_head, key_head, value_head, grad_head = items
        probs = head_probs(query_head, key_head, scale)
        probs16 = probs.astype(jnp.bfloat16)
        grad_probs = contract_last(grad_head, value_head)
        delta = jnp.sum(probs * grad_probs, axis=-1, keepdims=True)
        grad_scores = (probs * (grad_probs - delta)).astype(jnp.bfloat16)
        grad_q = (jnp.dot(grad_scores, key_head, preferred_element_type=jnp.float32) * scale).astype(jnp.bfloat16)
        grad_k = (contract_first(grad_scores, query_head) * scale).astype(jnp.bfloat16)
        grad_v = contract_first(probs16, grad_head).astype(jnp.bfloat16)
        return grad_q, grad_k, grad_v

    grad_q, grad_k, grad_v = lax.map(backward, (flat_q, flat_k, flat_v, grad_attn))
    shape = (CLIPS, HEADS, SEQ, DH)
    return grad_q.reshape(shape), grad_k.reshape(shape), grad_v.reshape(shape), grad_out_proj
```

```python
import functools

import jax
import jax.numpy as jnp
from jax import lax
from jax.experimental import pallas as pl
from jax.experimental.pallas import tpu as pltpu
from jax.sharding import PartitionSpec as P

AXES = ("hst", "seq")
LOG2E = 1.4426950408889634
CHUNKS = ((0, 1536), (1536, 3072))


def pairs(move):
    out = []
    for z in range(8):
        for y in range(4):
            for x in range(4):
                for core in range(2):
                    nx, ny, nc = move(x, y, core)
                    nx, ny = nx % 4, ny % 4
                    here = (z * 2 + y % 2) * 16 + x * 4 + (y // 2) * 2 + core
                    there = (z * 2 + ny % 2) * 16 + nx * 4 + (ny // 2) * 2 + nc
                    out.append((here, there))
    return out


FROM_X1 = pairs(lambda x, y, core: (x - 1, y, core))
FROM_X3 = pairs(lambda x, y, core: (x + 1, y, core))
FROM_X2 = pairs(lambda x, y, core: (x + 2, y, core))
SWAP_CORE = pairs(lambda x, y, core: (x, y, 1 - core))
SWAP_Y = pairs(lambda x, y, core: (x, y + 2, core))
MIRROR_Y = pairs(lambda x, y, core: (x, 3 - y, core))


def dot(left, right, left_dim, right_dim):
    return lax.dot_general(
        left, right, (((left_dim,), (right_dim,)), ((), ())), preferred_element_type=jnp.float32
    )


def forward_kernel(sub, scale, at_ref, q_ref, k_ref, v_ref, o_ref, inv_ref, p_ref):
    parts, _, rows, head_dim = q_ref.shape
    for part in range(parts):
        for start in range(0, rows, sub):
            here = pl.ds(part * rows + start, sub)
            scores = dot(q_ref[part, 0, pl.ds(start, sub), :], k_ref[...], 1, 1)
            row_max = jnp.max(scores, axis=1, keepdims=True)
            weights = jnp.exp2((scores - row_max) * (scale * LOG2E))
            inverse = 1.0 / jnp.sum(weights, axis=1, keepdims=True)
            weights16 = weights.astype(jnp.bfloat16)
            p_ref[here, :] = weights16
            o_ref[here, :] = (dot(weights16, v_ref[...], 1, 0) * inverse).astype(jnp.bfloat16)
            inv_ref[here, :] = jnp.broadcast_to(inverse, (sub, head_dim))


def forward_half(at, q4, keys, values):
    groups, _, rows, head_dim = q4.shape
    seq_len = keys.shape[0]
    half = groups * rows
    step = 2 * rows
    scale = 1.0 / head_dim**0.5
    block = lambda i, at: (i, 0)
    whole = lambda i, at: (0, 0)
    return pl.pallas_call(
        functools.partial(forward_kernel, 256, scale),
        grid_spec=pltpu.PrefetchScalarGridSpec(
            num_scalar_prefetch=1,
            grid=(groups // 2,),
            in_specs=[
                pl.BlockSpec((2, 1, rows, head_dim), lambda i, at: (i, at[0], 0, 0)),
                pl.BlockSpec((seq_len, head_dim), whole),
                pl.BlockSpec((seq_len, head_dim), whole),
            ],
            out_specs=[
                pl.BlockSpec((step, head_dim), block),
                pl.BlockSpec((step, head_dim), block),
                pl.BlockSpec((step, seq_len), block),
            ],
        ),
        out_shape=[
            jax.ShapeDtypeStruct((half, head_dim), jnp.bfloat16),
            jax.ShapeDtypeStruct((half, head_dim), jnp.float32),
            jax.ShapeDtypeStruct((half, seq_len), jnp.bfloat16),
        ],
        compiler_params=pltpu.CompilerParams(vmem_limit_bytes=30 << 20),
        cost_estimate=pl.CostEstimate(
            flops=5 * 10**9, bytes_accessed=6 << 20, transcendentals=half * seq_len
        ),
        name="attention_forward",
    )(at, q4, keys, values)


def backward_kernel(
    sub, scale, first, at_ref, q_ref, k_ref, v_ref, p_ref, g_ref, o_ref, inv_ref, *rest
):
    if first:
        dq_ref, dk_ref, dv_ref, dk_sum, dv_sum = rest
    else:
        dk_in, dv_in, _, dq_ref, dk_ref, dv_ref, dk_sum, dv_sum = rest
    step = pl.program_id(0)
    parts, _, rows, head_dim = q_ref.shape

    @pl.when(step == 0)
    def _():
        if first:
            dk_sum[...] = jnp.zeros_like(dk_sum)
            dv_sum[...] = jnp.zeros_like(dv_sum)
        else:
            dk_sum[...] = dk_in[...]
            dv_sum[...] = dv_in[...]

    for part in range(parts):
        for start in range(0, rows, sub):
            here = pl.ds(part * rows + start, sub)
            q_rows = q_ref[part, 0, pl.ds(start, sub), :]
            grad = g_ref[here, :].astype(jnp.float32) * inv_ref[here, :]
            grad16 = grad.astype(jnp.bfloat16)
            delta = jnp.sum(grad * o_ref[here, :].astype(jnp.float32), axis=1, keepdims=True)
            grad_probs = dot(grad16, v_ref[...], 1, 1)
            weights16 = p_ref[here, :]
            grad_scores = (weights16.astype(jnp.float32) * (grad_probs - delta)).astype(jnp.bfloat16)
            dq_ref[part, 0, pl.ds(start, sub), :] = (
                dot(grad_scores, k_ref[...], 1, 0) * scale
            ).astype(jnp.bfloat16)
            dk_sum[...] += dot(q_rows, grad_scores, 0, 0)
            dv_sum[...] += dot(grad16, weights16, 0, 0)

    @pl.when(step == pl.num_programs(0) - 1)
    def _():
        if first:
            dk_ref[...] = dk_sum[...]
            dv_ref[...] = dv_sum[...]
        else:
            dk_ref[...] = (dk_sum[...] * scale).T.astype(jnp.bfloat16)
            dv_ref[...] = dv_sum[...].T.astype(jnp.bfloat16)


def backward_half(at, q4, keys, values, weights, grad, attn, inverse, carry=None):
    groups, _, rows, head_dim = q4.shape
    seq_len = keys.shape[0]
    step = 2 * rows
    first = carry is None
    scale = 1.0 / head_dim**0.5
    block = lambda i, at: (i, 0)
    whole = lambda i, at: (0, 0)
    mine = pl.BlockSpec((2, 1, rows, head_dim), lambda i, at: (i, at[0], 0, 0))
    full = pl.BlockSpec((seq_len, head_dim), whole)
    flat = pl.BlockSpec((head_dim, seq_len), whole)
    rows_spec = pl.BlockSpec((step, head_dim), block)
    in_specs = [
        mine,
        full,
        full,
        pl.BlockSpec((step, seq_len), block),
        rows_spec,
        rows_spec,
        rows_spec,
    ]
    operands = [at, q4, keys, values, weights, grad, attn, inverse]
    dq_shape = jax.ShapeDtypeStruct(q4.shape, jnp.bfloat16)
    if first:
        out_specs = [mine, flat, flat]
        sums = jax.ShapeDtypeStruct((head_dim, seq_len), jnp.float32)
        aliases = {}
    else:
        in_specs += [flat, flat, pl.BlockSpec(memory_space=pl.ANY)]
        operands += [carry[1], carry[2], carry[0]]
        out_specs = [mine, full, full]
        sums = jax.ShapeDtypeStruct((seq_len, head_dim), jnp.bfloat16)
        aliases = {len(operands) - 1: 0}
    return pl.pallas_call(
        functools.partial(backward_kernel, 256, scale, first),
        grid_spec=pltpu.PrefetchScalarGridSpec(
            num_scalar_prefetch=1,
            grid=(groups // 2,),
            in_specs=in_specs,
            out_specs=out_specs,
            scratch_shapes=[
                pltpu.VMEM((head_dim, seq_len), jnp.float32),
                pltpu.VMEM((head_dim, seq_len), jnp.float32),
            ],
        ),
        out_shape=[dq_shape, sums, sums],
        input_output_aliases=aliases,
        compiler_params=pltpu.CompilerParams(vmem_limit_bytes=36 << 20),
        cost_estimate=pl.CostEstimate(flops=6 * 10**9, bytes_accessed=8 << 20, transcendentals=0),
        name="attention_backward",
    )(*operands)


def projection_kernel(place_ref, own_ref, other_ref, gate_ref, *refs):
    blocks, (own_out, other_out) = refs[:-2], refs[-2:]
    size = blocks[0].shape[0]
    tokens = jnp.concatenate([block[...] for block in blocks], axis=0)

    def rows(ref):
        return jnp.concatenate(
            [
                ref[pl.ds(pl.multiple_of(place_ref[slot] * size, size), size), :]
                for slot in range(len(blocks))
            ],
            axis=0,
        )

    gate = gate_ref[...]
    other_out[...] = (dot(rows(other_ref), tokens, 0, 0) * gate).astype(jnp.bfloat16)
    own_out[...] = (dot(rows(own_ref), tokens, 0, 0) * gate).astype(jnp.bfloat16)


def projection_grad(place, attn_own, attn_other, gate, blocks, tile=512):
    size, columns = blocks[0].shape
    half, head_dim = attn_own.shape
    tile = min(tile, columns)
    column = lambda i, place: (0, i)
    whole = pl.BlockSpec((half, head_dim), lambda i, place: (0, 0))
    out = jax.ShapeDtypeStruct((head_dim, columns), jnp.bfloat16)
    return pl.pallas_call(
        projection_kernel,
        grid_spec=pltpu.PrefetchScalarGridSpec(
            num_scalar_prefetch=1,
            grid=(columns // tile,),
            in_specs=[whole, whole, pl.BlockSpec((1, tile), column)]
            + [pl.BlockSpec((size, tile), column)] * len(blocks),
            out_specs=[pl.BlockSpec((head_dim, tile), column)] * 2,
        ),
        out_shape=[out, out],
        compiler_params=pltpu.CompilerParams(vmem_limit_bytes=24 << 20),
        cost_estimate=pl.CostEstimate(
            flops=4 * half * head_dim * columns, bytes_accessed=half * columns * 2, transcendentals=0
        ),
        name="projection_grad",
    )(place, attn_own, attn_other, gate, *blocks)


def tokens_kernel(counts, place_ref, weight_ref, *refs):
    blocks, (own_out, other_out, total) = refs[:-3], refs[-3:]
    step = pl.program_id(0)
    slots = len(blocks) // len(counts)
    size = blocks[0].shape[0]
    head_dim = own_out.shape[1]

    @pl.when(step == 0)
    def _():
        total[...] = jnp.zeros_like(total)

    start = 0
    for index, count in enumerate(counts):
        group = blocks[index * slots : (index + 1) * slots]

        @pl.when((step >= start) & (step < start + count))
        def _(group=group):
            tokens = jnp.concatenate([block[...] for block in group], axis=0)
            total[...] += dot(tokens, weight_ref[...], 1, 1)

        start += count

    @pl.when(step == pl.num_programs(0) - 1)
    def _():
        for slot in range(slots):
            here = pl.ds(pl.multiple_of(place_ref[slot] * size, size), size)
            rows = total[pl.ds(slot * size, size), :]
            own_out[here, :] = rows[:, :head_dim].astype(jnp.bfloat16)
            other_out[here, :] = rows[:, head_dim:].astype(jnp.bfloat16)


def tokens_grad(place, weight, groups, tile=512):
    size = groups[0][0].shape[0]
    slots = len(groups[0])
    heads = weight.shape[0]
    counts = [group[0].shape[1] // tile for group in groups]
    specs, blocks, start = [], [], 0
    for group, count in zip(groups, counts):
        index = lambda i, place, start=start, count=count: (0, jnp.clip(i - start, 0, count - 1))
        specs += [pl.BlockSpec((size, tile), index)] * slots
        blocks += list(group)
        start += count
    half = slots * size
    out = jax.ShapeDtypeStruct((half, heads // 2), jnp.bfloat16)
    whole = pl.BlockSpec((half, heads // 2), lambda i, place: (0, 0))
    return pl.pallas_call(
        functools.partial(tokens_kernel, counts),
        grid_spec=pltpu.PrefetchScalarGridSpec(
            num_scalar_prefetch=1,
            grid=(start,),
            in_specs=[pl.BlockSpec((heads, tile), lambda i, place: (0, i))] + specs,
            out_specs=[whole, whole],
            scratch_shapes=[pltpu.VMEM((half, heads), jnp.float32)],
        ),
        out_shape=[out, out],
        compiler_params=pltpu.CompilerParams(vmem_limit_bytes=30 << 20),
        cost_estimate=pl.CostEstimate(
            flops=2 * half * heads * tile * start, bytes_accessed=8 << 20, transcendentals=0
        ),
        name="tokens_grad",
    )(place, weight, *blocks)


def send(array, perm):
    return lax.ppermute(array, AXES, perm)


def shards(queries, keys, values, cotangent, gate, w_out):
    query_head, key_head, value_head = queries[0, 0], keys[0, 0], values[0, 0]
    seq_len, head_dim = query_head.shape
    seq = lax.axis_index("seq")
    x, y_hi, core = seq // 4, (seq // 2) % 2, seq % 2
    mine = jnp.reshape(y_hi, (1,)).astype(jnp.int32)
    theirs = 1 - mine
    place = jnp.stack(
        [((x + dx) % 4) * 2 + (core ^ e) for dx in range(4) for e in range(2)]
    ).astype(jnp.int32)
    q4 = query_head.reshape(4, 2, seq_len // 8, head_dim)

    groups = []
    for low, high in CHUNKS:
        block = cotangent[0][:, low:high]
        own = [block, send(block, FROM_X1), send(block, FROM_X2), send(block, FROM_X3)]
        groups.append([part for piece in own for part in (piece, send(piece, SWAP_CORE))])
    w_other = send(w_out, MIRROR_Y)
    weight = jnp.concatenate(
        [(w.astype(jnp.float32) * gate).astype(jnp.bfloat16) for w in (w_out, w_other)], axis=0
    )

    attn_theirs, inv_theirs, p_theirs = forward_half(theirs, q4, key_head, value_head)
    attn_other = send(attn_theirs, SWAP_Y)
    attn_mine, inv_mine, p_mine = forward_half(mine, q4, key_head, value_head)

    outs = []
    for (low, high), group in zip(CHUNKS, groups):
        own, other = projection_grad(place, attn_mine, attn_other, gate[:, low:high], group)
        columns = high - low
        summed = own.astype(jnp.float32) + send(other, SWAP_Y).astype(jnp.float32)
        pieces = summed.astype(jnp.bfloat16).reshape(16, head_dim // 16, columns)
        pieces = lax.all_to_all(pieces, "hst", 0, 0, tiled=True)
        piece = jnp.sum(pieces.astype(jnp.float32), axis=0).astype(jnp.bfloat16)
        everywhere = lax.all_to_all(
            jnp.broadcast_to(piece[None], (16,) + piece.shape), "hst", 0, 0, tiled=True
        )
        outs.append(everywhere.reshape(head_dim, columns).astype(jnp.float32))
    grad_out_proj = jnp.concatenate(outs, axis=1)

    grad_mine, grad_other = tokens_grad(place, weight, groups)
    grad_theirs = send(grad_other, SWAP_Y)
    carry = backward_half(
        mine, q4, key_head, value_head, p_mine, grad_mine, attn_mine, inv_mine
    )
    dq, dk, dv = backward_half(
        theirs, q4, key_head, value_head, p_theirs, grad_theirs, attn_theirs, inv_theirs, carry
    )
    return (
        dq.reshape(1, 1, seq_len, head_dim),
        dk[None, None],
        dv[None, None],
        grad_out_proj,
    )


def solution(mesh):
    in_specs = (
        P("hst", "seq", None, None),
        P("hst", "seq", None, None),
        P("hst", "seq", None, None),
        P("hst", "seq", None),
        P("hst", None),
        P("seq", None),
    )
    out_specs = (
        P("hst", "seq", None, None),
        P("hst", "seq", None, None),
        P("hst", "seq", None, None),
        P("seq", None),
    )
    return jax.shard_map(shards, mesh=mesh, in_specs=in_specs, out_specs=out_specs, check_vma=False)
```

```python
import functools

import jax
import jax.numpy as jnp
from jax import lax
from jax.experimental import pallas as pl
from jax.experimental.pallas import tpu as pltpu
from jax.sharding import PartitionSpec as P

AXES = ("hst", "seq")
LOG2E = 1.4426950408889634
SUB = 256
FORWARD_SUB = 512
TOKENS = 128
VMEM = 58 << 20
FULL_Y = tuple(
    tuple((z * 2 + y_lo) * 16 + x * 4 + y_hi * 2 + core for y_hi in range(2) for z in range(8) for y_lo in range(2))
    for x in range(4)
    for core in range(2)
)


def pairs(move):
    out = []
    for z in range(8):
        for y in range(4):
            for x in range(4):
                for core in range(2):
                    nx, ny, nc = move(x, y, core)
                    nx, ny = nx % 4, ny % 4
                    here = (z * 2 + y % 2) * 16 + x * 4 + (y // 2) * 2 + core
                    there = (z * 2 + ny % 2) * 16 + nx * 4 + (ny // 2) * 2 + nc
                    out.append((here, there))
    return out


FROM_X1 = pairs(lambda x, y, core: (x - 1, y, core))
FROM_X3 = pairs(lambda x, y, core: (x + 1, y, core))
FROM_X2 = pairs(lambda x, y, core: (x + 2, y, core))
SWAP_CORE = pairs(lambda x, y, core: (x, y, 1 - core))
SWAP_Y = pairs(lambda x, y, core: (x, y + 2, core))
MIRROR_Y = pairs(lambda x, y, core: (x, 3 - y, core))


def send(array, perm):
    return lax.ppermute(array, AXES, perm)


def dot(left, right, left_dim, right_dim):
    return lax.dot_general(
        left, right, (((left_dim,), (right_dim,)), ((), ())), preferred_element_type=jnp.float32
    )


def shape(*dims, dtype=jnp.bfloat16):
    return jax.ShapeDtypeStruct(dims, dtype)


def call(kernel, name, cost, out_shape, scalars, operands, scratch=(), out_any=(), inner=False):
    smem = [pl.BlockSpec(memory_space=pltpu.SMEM)] * len(scalars)
    space = pltpu.VMEM if inner else pl.ANY
    out_specs = [
        pl.BlockSpec(memory_space=pl.ANY if index in out_any else pltpu.VMEM)
        for index in range(len(out_shape))
    ]
    return pl.pallas_call(
        kernel,
        in_specs=smem + [pl.BlockSpec(memory_space=space)] * len(operands),
        out_specs=out_specs,
        out_shape=out_shape,
        scratch_shapes=list(scratch),
        compiler_params=pltpu.CompilerParams(vmem_limit_bytes=(12 << 20) if inner else VMEM),
        cost_estimate=pl.CostEstimate(flops=cost, bytes_accessed=1 << 18, transcendentals=0),
        name=name,
    )(*scalars, *operands)


def vmem(*dims, dtype=jnp.bfloat16):
    return pltpu.VMEM(dims, dtype)


class Loads:
    def __init__(self, sems):
        self.sems, self.copies = sems, []

    def start(self, source, target):
        copy = pltpu.make_async_copy(source, target, self.sems.at[len(self.copies)])
        copy.start()
        self.copies.append(copy)
        return copy


def forward_kernel(scale, q_in, k_in, v_in, o_ref, inv_ref, p_out, q_ref, k_ref, v_ref, p_ref, load_sems, store_sems):
    loads = Loads(load_sems)
    rows, head_dim = q_ref.shape
    queries = loads.start(q_in, q_ref)
    keys = loads.start(k_in, k_ref)
    values = loads.start(v_in, v_ref)
    queries.wait()
    keys.wait()
    stores = []
    ones = jnp.ones(v_ref.shape, jnp.bfloat16)
    for index, start in enumerate(range(0, rows, FORWARD_SUB)):
        here = pl.ds(start, FORWARD_SUB)
        scores = dot(q_ref[here, :], k_ref[...], 1, 1)
        row_max = jnp.max(scores, axis=1, keepdims=True)
        weights = jnp.exp2((scores - row_max) * (scale * LOG2E)).astype(jnp.bfloat16)
        p_ref[here, :] = weights
        store = pltpu.make_async_copy(p_ref.at[here], p_out.at[here], store_sems.at[index])
        store.start()
        stores.append(store)
        if start == 0:
            values.wait()
        both = dot(weights, jnp.concatenate([v_ref[...], ones], axis=1), 1, 0)
        inverse = 1.0 / both[:, head_dim:]
        o_ref[here, :] = (both[:, :head_dim] * inverse).astype(jnp.bfloat16)
        inv_ref[here, :] = inverse
    for store in stores:
        store.wait()


def forward(queries, keys, values):
    rows, head_dim = queries.shape
    count = keys.shape[0]
    return call(
        functools.partial(forward_kernel, 1.0 / head_dim**0.5),
        "attention_forward",
        5 * 10**8,
        [shape(rows, head_dim), shape(rows, head_dim, dtype=jnp.float32), shape(rows, count)],
        (),
        (queries, keys, values),
        [
            vmem(rows, head_dim),
            vmem(count, head_dim),
            vmem(count, head_dim),
            vmem(rows, count),
            pltpu.SemaphoreType.DMA((3,)),
            pltpu.SemaphoreType.DMA((rows // FORWARD_SUB,)),
        ],
        out_any=(2,),
    )


def backward_kernel(scale, groups, at_ref, *refs):
    ins, (dq_ref, dk_ref, dv_ref), held, sems = refs[:10], refs[10:13], refs[13:21], refs[21]
    q_ref, k_ref, v_ref, o_ref, inv_ref, p_ref, ga_ref, gb_ref = held
    rows = q_ref.shape[0]
    loads = Loads(sems)
    first = [loads.start(ins[index], target) for index, target in ((2, v_ref), (3, o_ref), (4, inv_ref))]
    for source, target, flip in ((6, ga_ref, 0), (8, gb_ref, 1)):
        for index, keys in enumerate(groups):
            start = 0
            for key in keys:
                there = ins[source + index].at[pl.ds(start, key[-1])]
                first.append(loads.start(there, target.at[rows_of(at_ref, key, flip)]))
                start += key[-1]
    parts = [pl.ds(index * SUB, SUB) for index in range(rows // SUB)]
    weights = []

    def load_weights(part):
        weights.append(loads.start(ins[5].at[parts[part]], p_ref.at[parts[part]]))

    load_weights(0)
    first += [loads.start(ins[1], k_ref), loads.start(ins[0], q_ref)]
    for part in range(1, len(parts)):
        load_weights(part)
    for copy in first:
        copy.wait()
    dk = dv = None
    for here, arrived in zip(parts, weights):
        grad = ga_ref[here, :].astype(jnp.float32) + gb_ref[here, :].astype(jnp.float32)
        grad = grad * inv_ref[here, :]
        grad16 = grad.astype(jnp.bfloat16)
        delta = jnp.sum(grad * o_ref[here, :].astype(jnp.float32), axis=1, keepdims=True)
        grad_probs = dot(grad16, v_ref[...], 1, 1)
        arrived.wait()
        weights16 = p_ref[here, :]
        grad_scores = (weights16.astype(jnp.float32) * (grad_probs - delta)).astype(jnp.bfloat16)
        dq_ref[here, :] = (dot(grad_scores, k_ref[...], 1, 0) * scale).astype(jnp.bfloat16)
        dk_part = dot(q_ref[here, :], grad_scores, 0, 0)
        dv_part = dot(grad16, weights16, 0, 0)
        dk = dk_part if dk is None else dk + dk_part
        dv = dv_part if dv is None else dv + dv_part
    dk_ref[...] = (dk * scale).T.astype(jnp.bfloat16)
    dv_ref[...] = dv.T.astype(jnp.bfloat16)


def backward(at, groups, queries, keys, values, attn, inverse, weights, own, got):
    rows, head_dim = queries.shape
    out = shape(rows, head_dim)
    copies = 5 + 2 * sum(len(keys) for keys in groups) + rows // SUB
    return call(
        functools.partial(backward_kernel, 1.0 / head_dim**0.5, groups),
        "attention_backward",
        10**9,
        [out, out, out],
        (at,),
        (queries, keys, values, attn, inverse, weights, *own, *got),
        [
            vmem(rows, head_dim),
            vmem(rows, head_dim),
            vmem(rows, head_dim),
            vmem(rows, head_dim),
            vmem(rows, head_dim, dtype=jnp.float32),
            vmem(rows, keys.shape[0]),
            vmem(rows, head_dim),
            vmem(rows, head_dim),
            pltpu.SemaphoreType.DMA((copies,)),
        ],
    )


def rows_of(at_ref, block, flip=0):
    dx, e, y, start, size = block
    x = lax.rem(at_ref[0] + dx, 4)
    y_hi = at_ref[1] if y == flip else 1 - at_ref[1]
    core = at_ref[2] if e == 0 else 1 - at_ref[2]
    return pl.ds(pl.multiple_of((x * 4 + y_hi * 2 + core) * TOKENS + start, size), size)


def load_tokens(loads, blocks, tokens):
    columns = tokens.shape[1] // 2
    parts = []
    for part in range(2):
        here = pl.ds(part * columns, columns)
        copies, start = [], 0
        for block in blocks:
            size = block.shape[0]
            copies.append(loads.start(block.at[:, here], tokens.at[pl.ds(start, size), here]))
            start += size
        parts.append((here, copies))
    return parts


def projection_kernel(keys, at_ref, *refs):
    count = len(keys)
    ins, rest = refs[:2], refs[2:]
    blocks, rest = rest[:count], rest[count:]
    last = len(rest) == 7
    if last:
        gate_in, sum_in, out_ref, heads, tokens, (gate_ref, sum_ref), sems = rest
    else:
        out_ref, heads, tokens, sems = rest
    loads = Loads(sems)
    head_dim = ins[0].shape[1]
    small, start = [], 0
    for key in keys:
        here = pl.ds(start, key[-1])
        start += key[-1]
        for index, ref in enumerate(ins):
            target = heads.at[here, pl.ds(index * head_dim, head_dim)]
            small.append(loads.start(ref.at[rows_of(at_ref, key)], target))
    parts = load_tokens(loads, blocks, tokens)
    if last:
        columns = tokens.shape[1]
        begin = pl.multiple_of(at_ref[1] * columns, columns)
        small += [loads.start(gate_in.at[:, pl.ds(begin, columns)], gate_ref), loads.start(sum_in, sum_ref)]
    for copy in small:
        copy.wait()
    for part, (here, copies) in enumerate(parts):
        for copy in copies:
            copy.wait()
        grad = dot(heads[...], tokens[:, here], 0, 0)
        if not last:
            out_ref[:, here] = grad
            continue
        grad = ((grad + sum_ref[:, here]) * gate_ref[:, here]).astype(jnp.bfloat16)
        for head in range(2):
            for row in range(0, head_dim, 16):
                first = head * head_dim + row
                out_ref[row // 16 * 2 + part, pl.ds(head * 16, 16), :] = grad[first : first + 16]


def projection_grad(at, keys, attn_own, attn_other, blocks, *last):
    head_dim, columns = attn_own.shape[1], blocks[0].shape[1]
    count = sum(key[-1] for key in keys)
    scratch = [vmem(count, 2 * head_dim), vmem(count, columns)]
    out = shape(2 * head_dim, columns, dtype=jnp.float32)
    if last:
        out = shape(16, 32, columns // 2)
        scratch.append([vmem(1, columns, dtype=jnp.float32), vmem(2 * head_dim, columns, dtype=jnp.float32)])
    return call(
        functools.partial(projection_kernel, keys),
        "projection_grad",
        10**8,
        [out],
        (at,),
        (attn_own, attn_other, *blocks, *last),
        scratch + [pltpu.SemaphoreType.DMA((2 + 4 * len(keys),))],
    )[0]


def tokens_kernel(count, at_ref, own_in, other_in, gate_in, *refs):
    blocks, (own_out, other_out, own_w, other_w, gate_ref, tokens, sems) = refs[:count], refs[count:]
    loads = Loads(sems)
    head_dim, columns = own_w.shape
    mine = pl.ds(pl.multiple_of(at_ref[1] * columns, columns), columns)
    small = [
        loads.start(own_in.at[:, mine], own_w),
        loads.start(other_in, other_w),
        loads.start(gate_in.at[:, mine], gate_ref),
    ]
    parts = load_tokens(loads, blocks, tokens)
    for copy in small:
        copy.wait()
    total = None
    for here, copies in parts:
        weight = jnp.concatenate(
            [
                (ref[:, here].astype(jnp.float32) * gate_ref[:, here]).astype(jnp.bfloat16)
                for ref in (own_w, other_w)
            ],
            axis=0,
        )
        for copy in copies:
            copy.wait()
        part = dot(tokens[:, here], weight, 1, 1)
        total = part if total is None else total + part
    own_out[...] = total[:, :head_dim].astype(jnp.bfloat16)
    other_out[...] = total[:, head_dim:].astype(jnp.bfloat16)


def tokens_grad(at, own_w, other_w, gate, blocks):
    rows = sum(block.shape[0] for block in blocks)
    head_dim, columns = other_w.shape
    out = shape(rows, head_dim)
    return call(
        functools.partial(tokens_kernel, len(blocks)),
        "tokens_grad",
        10**8,
        [out, out],
        (at,),
        (own_w, other_w, gate, *blocks),
        [
            vmem(head_dim, columns),
            vmem(head_dim, columns),
            vmem(1, columns, dtype=jnp.float32),
            vmem(rows, columns),
            pltpu.SemaphoreType.DMA((3 + 2 * len(blocks),)),
        ],
    )


def sum_kernel(at_ref, pieces_ref, out_ref):
    count = pieces_ref.shape[0]
    total = pieces_ref[0].astype(jnp.float32)
    for index in range(1, count):
        total += pieces_ref[index].astype(jnp.float32)
    total = total.astype(jnp.bfloat16)
    y_hi = at_ref[1]
    for index in range(count):
        out_ref[y_hi * count + index] = total[:16]
        out_ref[(1 - y_hi) * count + index] = total[16:]


def sum_pieces(at, pieces):
    count, rows, columns = pieces.shape
    out = [shape(2 * count, rows // 2, columns)]
    return call(sum_kernel, "sum_pieces", 10**7, out, (at,), (pieces,), inner=True)[0]


def place_kernel(pieces_ref, out_ref):
    count, size, columns = pieces_ref.shape
    for index in range(count):
        half, piece = divmod(index, count // 2)
        rows = pl.ds(piece // 2 * size, size)
        here = pl.ds((half * 2 + piece % 2) * columns, columns)
        out_ref[rows, here] = pieces_ref[index].astype(jnp.float32)


def place_pieces(pieces):
    count, size, columns = pieces.shape
    out = [shape(count // 4 * size, 4 * columns, dtype=jnp.float32)]
    return call(place_kernel, "place_pieces", 10**7, out, (), (pieces,), inner=True)[0]


def after(array, *others):
    return lax.optimization_barrier((array, *others))[0]


def shards(queries, keys, values, cotangent, gate, w_out):
    query_head, key_head, value_head = queries[0, 0], keys[0, 0], values[0, 0]
    half = gate.shape[1] // 2
    seq = lax.axis_index("seq")
    y_hi = (seq // 2) % 2

    def columns(array, y):
        return lax.dynamic_slice_in_dim(array, y * half, half, 1)

    keep = columns(cotangent[0], y_hi)
    near, far, across = [send(keep, perm) for perm in (FROM_X1, FROM_X3, FROM_X2)]
    got = send(columns(cotangent[0], 1 - y_hi), SWAP_Y)
    w_other = send(columns(w_out, 1 - y_hi), MIRROR_Y)
    attn, inverse, weights = forward(query_head, key_head, value_head)
    at = jnp.stack([seq // 4, y_hi, seq % 2]).astype(jnp.int32)

    near, far, across, got, w_other, _ = lax.optimization_barrier((near, far, across, got, w_other, attn))
    early = [keep, near, across, far]
    swapped = [send(part, SWAP_CORE) for part in early]
    got, attn_on, swapped = lax.optimization_barrier((got, attn, swapped))
    then = [got] + [send(got, perm) for perm in (FROM_X1, FROM_X2, FROM_X3)]
    attn_other = send(attn_on, SWAP_Y)

    def ends(y):
        return [(dx, e, y, 0, TOKENS) for dx in range(4) for e in range(2)]

    early = [part for pair in zip(early, swapped) for part in pair]
    own_1, other_1 = tokens_grad(at, w_out, w_other, gate, early)
    theirs_1 = send(other_1, SWAP_Y)
    partial = projection_grad(at, ends(0), after(attn, own_1), attn_other, early)
    then = lax.optimization_barrier((*then, partial))[:4]
    then = [part for block in then for part in (block, send(block, SWAP_CORE))]
    pieces = projection_grad(at, ends(1), attn, attn_other, then, gate, partial)
    own_2, other_2 = tokens_grad(at, after(w_out, pieces), w_other, gate, then)
    theirs_2 = send(other_2, SWAP_Y)
    pieces = lax.all_to_all(after(pieces, theirs_1), "hst", 0, 0, tiled=True)
    summed = sum_pieces(at, after(pieces, theirs_2))
    dq, dk, dv = backward(
        at,
        (ends(0), ends(1)),
        query_head,
        key_head,
        value_head,
        attn,
        inverse,
        weights,
        (after(own_1, summed), own_2),
        (theirs_1, theirs_2),
    )
    everywhere = lax.all_to_all(summed, AXES, 0, 0, tiled=True, axis_index_groups=FULL_Y)
    grad_out_proj = place_pieces(everywhere)
    return dq[None, None], dk[None, None], dv[None, None], grad_out_proj


def solution(mesh):
    in_specs = (
        P("hst", "seq", None, None),
        P("hst", "seq", None, None),
        P("hst", "seq", None, None),
        P("hst", "seq", None),
        P("hst", None),
        P("seq", None),
    )
    out_specs = (
        P("hst", "seq", None, None),
        P("hst", "seq", None, None),
        P("hst", "seq", None, None),
        P("seq", None),
    )
    return jax.shard_map(shards, mesh=mesh, in_specs=in_specs, out_specs=out_specs, check_vma=False)
```

```python
import functools

import jax
import jax.numpy as jnp
from jax import lax
from jax.experimental import pallas as pl
from jax.experimental.pallas import tpu as pltpu
from jax.sharding import PartitionSpec as P

AXES = ("hst", "seq")
LOG2E = 1.4426950408889634
SUB = 256
FORWARD_SUB = 512
TOKENS = 128
VMEM = 58 << 20
FULL_Y = tuple(
    tuple((z * 2 + y_lo) * 16 + x * 4 + y_hi * 2 + core for y_hi in range(2) for z in range(8) for y_lo in range(2))
    for x in range(4)
    for core in range(2)
)


def pairs(move):
    out = []
    for z in range(8):
        for y in range(4):
            for x in range(4):
                for core in range(2):
                    nx, ny, nc = move(x, y, core)
                    nx, ny = nx % 4, ny % 4
                    here = (z * 2 + y % 2) * 16 + x * 4 + (y // 2) * 2 + core
                    there = (z * 2 + ny % 2) * 16 + nx * 4 + (ny // 2) * 2 + nc
                    out.append((here, there))
    return out


FROM_X1 = pairs(lambda x, y, core: (x - 1, y, core))
FROM_X3 = pairs(lambda x, y, core: (x + 1, y, core))
FROM_X2 = pairs(lambda x, y, core: (x + 2, y, core))
SWAP_CORE = pairs(lambda x, y, core: (x, y, 1 - core))
SWAP_Y = pairs(lambda x, y, core: (x, y + 2, core))
MIRROR_Y = pairs(lambda x, y, core: (x, 3 - y, core))


def send(array, perm):
    return lax.ppermute(array, AXES, perm)


def dot(left, right, left_dim, right_dim):
    return lax.dot_general(
        left, right, (((left_dim,), (right_dim,)), ((), ())), preferred_element_type=jnp.float32
    )


def shape(*dims, dtype=jnp.bfloat16):
    return jax.ShapeDtypeStruct(dims, dtype)


def call(kernel, name, cost, out_shape, scalars, operands, scratch=(), out_any=(), inner=False, limit=VMEM):
    smem = [pl.BlockSpec(memory_space=pltpu.SMEM)] * len(scalars)
    space = pltpu.VMEM if inner else pl.ANY
    out_specs = [
        pl.BlockSpec(memory_space=pl.ANY if index in out_any else pltpu.VMEM)
        for index in range(len(out_shape))
    ]
    return pl.pallas_call(
        kernel,
        in_specs=smem + [pl.BlockSpec(memory_space=space)] * len(operands),
        out_specs=out_specs,
        out_shape=out_shape,
        scratch_shapes=list(scratch),
        compiler_params=pltpu.CompilerParams(vmem_limit_bytes=(12 << 20) if inner else limit),
        cost_estimate=pl.CostEstimate(flops=cost, bytes_accessed=1 << 18, transcendentals=0),
        name=name,
    )(*scalars, *operands)


def vmem(*dims, dtype=jnp.bfloat16):
    return pltpu.VMEM(dims, dtype)


class Loads:
    def __init__(self, sems):
        self.sems, self.copies = sems, []

    def start(self, source, target):
        copy = pltpu.make_async_copy(source, target, self.sems.at[len(self.copies)])
        copy.start()
        self.copies.append(copy)
        return copy


def forward_kernel(scale, q_in, k_in, v_in, o_ref, inv_ref, p_out, q_ref, k_ref, v_ref, p_ref, load_sems, store_sems):
    loads = Loads(load_sems)
    rows, head_dim = q_ref.shape
    queries = loads.start(q_in, q_ref)
    keys = loads.start(k_in, k_ref)
    values = loads.start(v_in, v_ref)
    queries.wait()
    keys.wait()
    stores = []
    ones = jnp.ones(v_ref.shape, jnp.bfloat16)
    for index, start in enumerate(range(0, rows, FORWARD_SUB)):
        here = pl.ds(start, FORWARD_SUB)
        scores = dot(q_ref[here, :], k_ref[...], 1, 1)
        row_max = jnp.max(scores, axis=1, keepdims=True)
        weights = jnp.exp2((scores - row_max) * (scale * LOG2E)).astype(jnp.bfloat16)
        p_ref[here, :] = weights
        store = pltpu.make_async_copy(p_ref.at[here], p_out.at[here], store_sems.at[index])
        store.start()
        stores.append(store)
        if start == 0:
            values.wait()
        both = dot(weights, jnp.concatenate([v_ref[...], ones], axis=1), 1, 0)
        inverse = 1.0 / both[:, head_dim:]
        o_ref[here, :] = (both[:, :head_dim] * inverse).astype(jnp.bfloat16)
        inv_ref[here, :] = inverse
    for store in stores:
        store.wait()


def forward(queries, keys, values):
    rows, head_dim = queries.shape
    count = keys.shape[0]
    return call(
        functools.partial(forward_kernel, 1.0 / head_dim**0.5),
        "attention_forward",
        5 * 10**8,
        [shape(rows, head_dim), shape(rows, head_dim, dtype=jnp.float32), shape(rows, count)],
        (),
        (queries, keys, values),
        [
            vmem(rows, head_dim),
            vmem(count, head_dim),
            vmem(count, head_dim),
            vmem(rows, count),
            pltpu.SemaphoreType.DMA((3,)),
            pltpu.SemaphoreType.DMA((rows // FORWARD_SUB,)),
        ],
        out_any=(2,),
    )


def backward_kernel(scale, groups, at_ref, *refs):
    ins, (dq_ref, dk_ref, dv_ref), held, sems = refs[:10], refs[10:13], refs[13:21], refs[21]
    q_ref, k_ref, v_ref, o_ref, inv_ref, p_ref, ga_ref, gb_ref = held
    rows = q_ref.shape[0]
    loads = Loads(sems)
    first = [loads.start(ins[index], target) for index, target in ((2, v_ref), (3, o_ref), (4, inv_ref))]
    for source, target, flip in ((6, ga_ref, 0), (8, gb_ref, 1)):
        for index, keys in enumerate(groups):
            start = 0
            for key in keys:
                there = ins[source + index].at[pl.ds(start, key[-1])]
                first.append(loads.start(there, target.at[rows_of(at_ref, key, flip)]))
                start += key[-1]
    parts = [pl.ds(index * SUB, SUB) for index in range(rows // SUB)]
    weights = []

    def load_weights(part):
        weights.append(loads.start(ins[5].at[parts[part]], p_ref.at[parts[part]]))

    load_weights(0)
    first += [loads.start(ins[1], k_ref), loads.start(ins[0], q_ref)]
    for part in range(1, len(parts)):
        load_weights(part)
    for copy in first:
        copy.wait()
    dk = dv = None
    for here, arrived in zip(parts, weights):
        grad = ga_ref[here, :].astype(jnp.float32) + gb_ref[here, :].astype(jnp.float32)
        grad = grad * inv_ref[here, :]
        grad16 = grad.astype(jnp.bfloat16)
        delta = jnp.sum(grad * o_ref[here, :].astype(jnp.float32), axis=1, keepdims=True)
        grad_probs = dot(grad16, v_ref[...], 1, 1)
        arrived.wait()
        weights16 = p_ref[here, :]
        grad_scores = (weights16.astype(jnp.float32) * (grad_probs - delta)).astype(jnp.bfloat16)
        dq_ref[here, :] = (dot(grad_scores, k_ref[...], 1, 0) * scale).astype(jnp.bfloat16)
        dk_part = dot(q_ref[here, :], grad_scores, 0, 0)
        dv_part = dot(grad16, weights16, 0, 0)
        dk = dk_part if dk is None else dk + dk_part
        dv = dv_part if dv is None else dv + dv_part
    dk_ref[...] = (dk * scale).T.astype(jnp.bfloat16)
    dv_ref[...] = dv.T.astype(jnp.bfloat16)


def backward(at, groups, queries, keys, values, attn, inverse, weights, own, got):
    rows, head_dim = queries.shape
    out = shape(rows, head_dim)
    copies = 5 + 2 * sum(len(keys) for keys in groups) + rows // SUB
    return call(
        functools.partial(backward_kernel, 1.0 / head_dim**0.5, groups),
        "attention_backward",
        10**9,
        [out, out, out],
        (at,),
        (queries, keys, values, attn, inverse, weights, *own, *got),
        [
            vmem(rows, head_dim),
            vmem(rows, head_dim),
            vmem(rows, head_dim),
            vmem(rows, head_dim),
            vmem(rows, head_dim, dtype=jnp.float32),
            vmem(rows, keys.shape[0]),
            vmem(rows, head_dim),
            vmem(rows, head_dim),
            pltpu.SemaphoreType.DMA((copies,)),
        ],
    )


def rows_of(at_ref, block, flip=0):
    dx, e, y, start, size = block
    x = lax.rem(at_ref[0] + dx, 4)
    y_hi = at_ref[1] if y == flip else 1 - at_ref[1]
    core = at_ref[2] if e == 0 else 1 - at_ref[2]
    return pl.ds(pl.multiple_of((x * 4 + y_hi * 2 + core) * TOKENS + start, size), size)


def load_tokens(loads, blocks, tokens):
    columns = tokens.shape[1] // 2
    parts = []
    for part in range(2):
        here = pl.ds(part * columns, columns)
        copies, start = [], 0
        for block in blocks:
            size = block.shape[0]
            copies.append(loads.start(block.at[:, here], tokens.at[pl.ds(start, size), here]))
            start += size
        parts.append((here, copies))
    return parts


def projection_kernel(keys, at_ref, *refs):
    count = len(keys)
    ins, rest = refs[:2], refs[2:]
    blocks, rest = rest[:count], rest[count:]
    last = len(rest) == 7
    if last:
        gate_in, sum_in, out_ref, heads, tokens, (gate_ref, sum_ref), sems = rest
    else:
        out_ref, heads, tokens, sems = rest
    loads = Loads(sems)
    head_dim = ins[0].shape[1]
    small, start = [], 0
    for key in keys:
        here = pl.ds(start, key[-1])
        start += key[-1]
        for index, ref in enumerate(ins):
            target = heads.at[here, pl.ds(index * head_dim, head_dim)]
            small.append(loads.start(ref.at[rows_of(at_ref, key)], target))
    parts = load_tokens(loads, blocks, tokens)
    if last:
        columns = tokens.shape[1]
        begin = pl.multiple_of(at_ref[1] * columns, columns)
        small += [loads.start(gate_in.at[:, pl.ds(begin, columns)], gate_ref), loads.start(sum_in, sum_ref)]
    for copy in small:
        copy.wait()
    for part, (here, copies) in enumerate(parts):
        for copy in copies:
            copy.wait()
        grad = dot(heads[...], tokens[:, here], 0, 0)
        if not last:
            out_ref[:, here] = grad
            continue
        grad = ((grad + sum_ref[:, here]) * gate_ref[:, here]).astype(jnp.bfloat16)
        for head in range(2):
            for row in range(0, head_dim, 16):
                first = head * head_dim + row
                out_ref[row // 16 * 2 + part, pl.ds(head * 16, 16), :] = grad[first : first + 16]


def projection_grad(at, keys, attn_own, attn_other, blocks, *last):
    head_dim, columns = attn_own.shape[1], blocks[0].shape[1]
    count = sum(key[-1] for key in keys)
    scratch = [vmem(count, 2 * head_dim), vmem(count, columns)]
    out = shape(2 * head_dim, columns, dtype=jnp.float32)
    if last:
        out = shape(16, 32, columns // 2)
        scratch.append([vmem(1, columns, dtype=jnp.float32), vmem(2 * head_dim, columns, dtype=jnp.float32)])
    return call(
        functools.partial(projection_kernel, keys),
        "projection_grad",
        10**8,
        [out],
        (at,),
        (attn_own, attn_other, *blocks, *last),
        scratch + [pltpu.SemaphoreType.DMA((2 + 4 * len(keys),))],
        limit=(20 << 20) if last else VMEM,
    )[0]


def tokens_kernel(count, at_ref, own_in, other_in, gate_in, *refs):
    blocks, (own_out, other_out, own_w, other_w, gate_ref, tokens, sems) = refs[:count], refs[count:]
    loads = Loads(sems)
    head_dim, columns = own_w.shape
    mine = pl.ds(pl.multiple_of(at_ref[1] * columns, columns), columns)
    small = [
        loads.start(own_in.at[:, mine], own_w),
        loads.start(other_in, other_w),
        loads.start(gate_in.at[:, mine], gate_ref),
    ]
    parts = load_tokens(loads, blocks, tokens)
    for copy in small:
        copy.wait()
    total = None
    for here, copies in parts:
        weight = jnp.concatenate(
            [
                (ref[:, here].astype(jnp.float32) * gate_ref[:, here]).astype(jnp.bfloat16)
                for ref in (own_w, other_w)
            ],
            axis=0,
        )
        for copy in copies:
            copy.wait()
        part = dot(tokens[:, here], weight, 1, 1)
        total = part if total is None else total + part
    own_out[...] = total[:, :head_dim].astype(jnp.bfloat16)
    other_out[...] = total[:, head_dim:].astype(jnp.bfloat16)


def tokens_grad(at, own_w, other_w, gate, blocks):
    rows = sum(block.shape[0] for block in blocks)
    head_dim, columns = other_w.shape
    out = shape(rows, head_dim)
    return call(
        functools.partial(tokens_kernel, len(blocks)),
        "tokens_grad",
        10**8,
        [out, out],
        (at,),
        (own_w, other_w, gate, *blocks),
        [
            vmem(head_dim, columns),
            vmem(head_dim, columns),
            vmem(1, columns, dtype=jnp.float32),
            vmem(rows, columns),
            pltpu.SemaphoreType.DMA((3 + 2 * len(blocks),)),
        ],
    )


def sum_kernel(at_ref, pieces_ref, out_ref):
    count = pieces_ref.shape[0]
    total = pieces_ref[0].astype(jnp.float32)
    for index in range(1, count):
        total += pieces_ref[index].astype(jnp.float32)
    total = total.astype(jnp.bfloat16)
    y_hi = at_ref[1]
    for index in range(count):
        out_ref[y_hi * count + index] = total[:16]
        out_ref[(1 - y_hi) * count + index] = total[16:]


def sum_pieces(at, pieces):
    count, rows, columns = pieces.shape
    out = [shape(2 * count, rows // 2, columns)]
    return call(sum_kernel, "sum_pieces", 10**7, out, (at,), (pieces,), inner=True)[0]


def place_kernel(pieces_ref, out_ref):
    count, size, columns = pieces_ref.shape
    for index in range(count):
        half, piece = divmod(index, count // 2)
        rows = pl.ds(piece // 2 * size, size)
        here = pl.ds((half * 2 + piece % 2) * columns, columns)
        out_ref[rows, here] = pieces_ref[index].astype(jnp.float32)


def place_pieces(pieces):
    count, size, columns = pieces.shape
    out = [shape(count // 4 * size, 4 * columns, dtype=jnp.float32)]
    return call(place_kernel, "place_pieces", 10**7, out, (), (pieces,), inner=True)[0]


def after(array, *others):
    return lax.optimization_barrier((array, *others))[0]


def shards(queries, keys, values, cotangent, gate, w_out):
    query_head, key_head, value_head = queries[0, 0], keys[0, 0], values[0, 0]
    half = gate.shape[1] // 2
    seq = lax.axis_index("seq")
    y_hi = (seq // 2) % 2

    def columns(array, y):
        return lax.dynamic_slice_in_dim(array, y * half, half, 1)

    keep = columns(cotangent[0], y_hi)
    near, far, across = [send(keep, perm) for perm in (FROM_X1, FROM_X3, FROM_X2)]
    got = send(columns(cotangent[0], 1 - y_hi), SWAP_Y)
    w_other = send(columns(w_out, 1 - y_hi), MIRROR_Y)
    attn, inverse, weights = forward(query_head, key_head, value_head)
    at = jnp.stack([seq // 4, y_hi, seq % 2]).astype(jnp.int32)

    near, far, across, got, w_other, attn_on = lax.optimization_barrier((near, far, across, got, w_other, attn))
    early = [keep, near, across, far]
    swapped = [send(part, SWAP_CORE) for part in early]
    then = [got] + [send(got, perm) for perm in (FROM_X1, FROM_X2, FROM_X3)]
    attn_other = send(attn_on, SWAP_Y)

    def ends(y):
        return [(dx, e, y, 0, TOKENS) for dx in range(4) for e in range(2)]

    early = [part for pair in zip(early, swapped) for part in pair]
    own_1, other_1 = tokens_grad(at, w_out, w_other, gate, early)
    theirs_1 = send(other_1, SWAP_Y)
    partial = projection_grad(at, ends(0), after(attn, own_1), attn_other, early)
    then = lax.optimization_barrier((*then, partial))[:4]
    then = [part for block in then for part in (block, send(block, SWAP_CORE))]
    pieces = projection_grad(at, ends(1), attn, attn_other, then, gate, partial)
    own_2, other_2 = tokens_grad(at, after(w_out, pieces), w_other, gate, then)
    theirs_2 = send(other_2, SWAP_Y)
    pieces = lax.all_to_all(after(pieces, theirs_1), "hst", 0, 0, tiled=True)
    summed = sum_pieces(at, after(pieces, theirs_2))
    dq, dk, dv = backward(
        at,
        (ends(0), ends(1)),
        query_head,
        key_head,
        value_head,
        attn,
        inverse,
        weights,
        (after(own_1, summed), own_2),
        (theirs_1, theirs_2),
    )
    everywhere = lax.all_to_all(summed, AXES, 0, 0, tiled=True, axis_index_groups=FULL_Y)
    grad_out_proj = place_pieces(everywhere)
    return dq[None, None], dk[None, None], dv[None, None], grad_out_proj


def solution(mesh):
    in_specs = (
        P("hst", "seq", None, None),
        P("hst", "seq", None, None),
        P("hst", "seq", None, None),
        P("hst", "seq", None),
        P("hst", None),
        P("seq", None),
    )
    out_specs = (
        P("hst", "seq", None, None),
        P("hst", "seq", None, None),
        P("hst", "seq", None, None),
        P("seq", None),
    )
    return jax.shard_map(shards, mesh=mesh, in_specs=in_specs, out_specs=out_specs, check_vma=False)
```

```python
import functools

import jax
import jax.numpy as jnp
from jax import lax
from jax.experimental import pallas as pl
from jax.experimental.pallas import tpu as pltpu
from jax.sharding import PartitionSpec as P

AXES = ("hst", "seq")
LOG2E = 1.4426950408889634
SUB = 256
FORWARD_SUB = 512
TOKENS = 128
VMEM = 58 << 20
FULL_Y = tuple(
    tuple((z * 2 + y_lo) * 16 + x * 4 + y_hi * 2 + core for y_hi in range(2) for z in range(8) for y_lo in range(2))
    for x in range(4)
    for core in range(2)
)


def pairs(move):
    out = []
    for z in range(8):
        for y in range(4):
            for x in range(4):
                for core in range(2):
                    nx, ny, nc = move(x, y, core)
                    nx, ny = nx % 4, ny % 4
                    here = (z * 2 + y % 2) * 16 + x * 4 + (y // 2) * 2 + core
                    there = (z * 2 + ny % 2) * 16 + nx * 4 + (ny // 2) * 2 + nc
                    out.append((here, there))
    return out


FROM_X1 = pairs(lambda x, y, core: (x - 1, y, core))
FROM_X3 = pairs(lambda x, y, core: (x + 1, y, core))
FROM_X2 = pairs(lambda x, y, core: (x + 2, y, core))
SWAP_CORE = pairs(lambda x, y, core: (x, y, 1 - core))
SWAP_Y = pairs(lambda x, y, core: (x, y + 2, core))
MIRROR_Y = pairs(lambda x, y, core: (x, 3 - y, core))


def send(array, perm):
    return lax.ppermute(array, AXES, perm)


def dot(left, right, left_dim, right_dim):
    return lax.dot_general(
        left, right, (((left_dim,), (right_dim,)), ((), ())), preferred_element_type=jnp.float32
    )


def shape(*dims, dtype=jnp.bfloat16):
    return jax.ShapeDtypeStruct(dims, dtype)


def call(kernel, name, cost, out_shape, scalars, operands, scratch=(), out_any=(), inner=False, limit=VMEM):
    smem = [pl.BlockSpec(memory_space=pltpu.SMEM)] * len(scalars)
    space = pltpu.VMEM if inner else pl.ANY
    out_specs = [
        pl.BlockSpec(memory_space=pl.ANY if index in out_any else pltpu.VMEM)
        for index in range(len(out_shape))
    ]
    return pl.pallas_call(
        kernel,
        in_specs=smem + [pl.BlockSpec(memory_space=space)] * len(operands),
        out_specs=out_specs,
        out_shape=out_shape,
        scratch_shapes=list(scratch),
        compiler_params=pltpu.CompilerParams(vmem_limit_bytes=(12 << 20) if inner else limit),
        cost_estimate=pl.CostEstimate(flops=cost, bytes_accessed=1 << 18, transcendentals=0),
        name=name,
    )(*scalars, *operands)


def vmem(*dims, dtype=jnp.bfloat16):
    return pltpu.VMEM(dims, dtype)


class Loads:
    def __init__(self, sems):
        self.sems, self.copies = sems, []

    def start(self, source, target):
        copy = pltpu.make_async_copy(source, target, self.sems.at[len(self.copies)])
        copy.start()
        self.copies.append(copy)
        return copy


def forward_kernel(scale, q_in, k_in, v_in, o_ref, inv_ref, p_out, q_ref, k_ref, v_ref, p_ref, load_sems, store_sems):
    loads = Loads(load_sems)
    rows, head_dim = q_ref.shape
    queries = loads.start(q_in, q_ref)
    keys = loads.start(k_in, k_ref)
    values = loads.start(v_in, v_ref)
    queries.wait()
    keys.wait()
    stores = []
    ones = jnp.ones(v_ref.shape, jnp.bfloat16)
    for index, start in enumerate(range(0, rows, FORWARD_SUB)):
        here = pl.ds(start, FORWARD_SUB)
        scores = dot(q_ref[here, :], k_ref[...], 1, 1)
        row_max = jnp.max(scores, axis=1, keepdims=True)
        weights = jnp.exp2((scores - row_max) * (scale * LOG2E)).astype(jnp.bfloat16)
        p_ref[here, :] = weights
        store = pltpu.make_async_copy(p_ref.at[here], p_out.at[here], store_sems.at[index])
        store.start()
        stores.append(store)
        if start == 0:
            values.wait()
        both = dot(weights, jnp.concatenate([v_ref[...], ones], axis=1), 1, 0)
        inverse = 1.0 / both[:, head_dim:]
        o_ref[here, :] = (both[:, :head_dim] * inverse).astype(jnp.bfloat16)
        inv_ref[here, :] = inverse
    for store in stores:
        store.wait()


def forward(queries, keys, values):
    rows, head_dim = queries.shape
    count = keys.shape[0]
    return call(
        functools.partial(forward_kernel, 1.0 / head_dim**0.5),
        "attention_forward",
        5 * 10**8,
        [shape(rows, head_dim), shape(rows, head_dim, dtype=jnp.float32), shape(rows, count)],
        (),
        (queries, keys, values),
        [
            vmem(rows, head_dim),
            vmem(count, head_dim),
            vmem(count, head_dim),
            vmem(rows, count),
            pltpu.SemaphoreType.DMA((3,)),
            pltpu.SemaphoreType.DMA((rows // FORWARD_SUB,)),
        ],
        out_any=(2,),
    )


def backward_kernel(scale, groups, at_ref, *refs):
    ins, (dq_ref, dk_ref, dv_ref), held, sems = refs[:10], refs[10:13], refs[13:21], refs[21]
    q_ref, k_ref, v_ref, o_ref, inv_ref, p_ref, ga_ref, gb_ref = held
    rows = q_ref.shape[0]
    loads = Loads(sems)
    first = [loads.start(ins[index], target) for index, target in ((2, v_ref), (3, o_ref), (4, inv_ref))]
    for source, target, flip in ((6, ga_ref, 0), (8, gb_ref, 1)):
        for index, keys in enumerate(groups):
            start = 0
            for key in keys:
                there = ins[source + index].at[pl.ds(start, key[-1])]
                first.append(loads.start(there, target.at[rows_of(at_ref, key, flip)]))
                start += key[-1]
    parts = [pl.ds(index * SUB, SUB) for index in range(rows // SUB)]
    weights = []

    def load_weights(part):
        weights.append(loads.start(ins[5].at[parts[part]], p_ref.at[parts[part]]))

    load_weights(0)
    first += [loads.start(ins[1], k_ref), loads.start(ins[0], q_ref)]
    for part in range(1, len(parts)):
        load_weights(part)
    for copy in first:
        copy.wait()
    dk = dv = None
    for here, arrived in zip(parts, weights):
        grad = ga_ref[here, :].astype(jnp.float32) + gb_ref[here, :].astype(jnp.float32)
        grad = grad * inv_ref[here, :]
        grad16 = grad.astype(jnp.bfloat16)
        delta = jnp.sum(grad * o_ref[here, :].astype(jnp.float32), axis=1, keepdims=True)
        grad_probs = dot(grad16, v_ref[...], 1, 1)
        arrived.wait()
        weights16 = p_ref[here, :]
        grad_scores = (weights16.astype(jnp.float32) * (grad_probs - delta)).astype(jnp.bfloat16)
        dq_ref[here, :] = (dot(grad_scores, k_ref[...], 1, 0) * scale).astype(jnp.bfloat16)
        dk_part = dot(q_ref[here, :], grad_scores, 0, 0)
        dv_part = dot(grad16, weights16, 0, 0)
        dk = dk_part if dk is None else dk + dk_part
        dv = dv_part if dv is None else dv + dv_part
    dk_ref[...] = (dk * scale).T.astype(jnp.bfloat16)
    dv_ref[...] = dv.T.astype(jnp.bfloat16)


def backward(at, groups, queries, keys, values, attn, inverse, weights, own, got):
    rows, head_dim = queries.shape
    out = shape(rows, head_dim)
    copies = 5 + 2 * sum(len(keys) for keys in groups) + rows // SUB
    return call(
        functools.partial(backward_kernel, 1.0 / head_dim**0.5, groups),
        "attention_backward",
        10**9,
        [out, out, out],
        (at,),
        (queries, keys, values, attn, inverse, weights, *own, *got),
        [
            vmem(rows, head_dim),
            vmem(rows, head_dim),
            vmem(rows, head_dim),
            vmem(rows, head_dim),
            vmem(rows, head_dim, dtype=jnp.float32),
            vmem(rows, keys.shape[0]),
            vmem(rows, head_dim),
            vmem(rows, head_dim),
            pltpu.SemaphoreType.DMA((copies,)),
        ],
    )


def rows_of(at_ref, block, flip=0):
    dx, e, y, start, size = block
    x = lax.rem(at_ref[0] + dx, 4)
    y_hi = at_ref[1] if y == flip else 1 - at_ref[1]
    core = at_ref[2] if e == 0 else 1 - at_ref[2]
    return pl.ds(pl.multiple_of((x * 4 + y_hi * 2 + core) * TOKENS + start, size), size)


def load_tokens(loads, blocks, tokens):
    columns = tokens.shape[1] // 2
    parts = []
    for part in range(2):
        here = pl.ds(part * columns, columns)
        copies, start = [], 0
        for block in blocks:
            size = block.shape[0]
            copies.append(loads.start(block.at[:, here], tokens.at[pl.ds(start, size), here]))
            start += size
        parts.append((here, copies))
    return parts


def projection_kernel(keys, at_ref, *refs):
    count = len(keys)
    ins, rest = refs[:2], refs[2:]
    blocks, rest = rest[:count], rest[count:]
    last = len(rest) == 7
    if last:
        gate_in, sum_in, out_ref, heads, tokens, (gate_ref, sum_ref), sems = rest
    else:
        out_ref, heads, tokens, sems = rest
    loads = Loads(sems)
    head_dim = ins[0].shape[1]
    small, start = [], 0
    for key in keys:
        here = pl.ds(start, key[-1])
        start += key[-1]
        for index, ref in enumerate(ins):
            target = heads.at[here, pl.ds(index * head_dim, head_dim)]
            small.append(loads.start(ref.at[rows_of(at_ref, key)], target))
    parts = load_tokens(loads, blocks, tokens)
    if last:
        columns = tokens.shape[1]
        begin = pl.multiple_of(at_ref[1] * columns, columns)
        small += [loads.start(gate_in.at[:, pl.ds(begin, columns)], gate_ref), loads.start(sum_in, sum_ref)]
    for copy in small:
        copy.wait()
    for part, (here, copies) in enumerate(parts):
        for copy in copies:
            copy.wait()
        grad = dot(heads[...], tokens[:, here], 0, 0)
        if not last:
            out_ref[:, here] = grad
            continue
        grad = ((grad + sum_ref[:, here]) * gate_ref[:, here]).astype(jnp.bfloat16)
        for head in range(2):
            for row in range(0, head_dim, 16):
                first = head * head_dim + row
                out_ref[row // 16 * 2 + part, pl.ds(head * 16, 16), :] = grad[first : first + 16]


def projection_grad(at, keys, attn_own, attn_other, blocks, *last):
    head_dim, columns = attn_own.shape[1], blocks[0].shape[1]
    count = sum(key[-1] for key in keys)
    scratch = [vmem(count, 2 * head_dim), vmem(count, columns)]
    out = shape(2 * head_dim, columns, dtype=jnp.float32)
    if last:
        out = shape(16, 32, columns // 2)
        scratch.append([vmem(1, columns, dtype=jnp.float32), vmem(2 * head_dim, columns, dtype=jnp.float32)])
    return call(
        functools.partial(projection_kernel, keys),
        "projection_grad",
        10**8,
        [out],
        (at,),
        (attn_own, attn_other, *blocks, *last),
        scratch + [pltpu.SemaphoreType.DMA((2 + 4 * len(keys),))],
        limit=(20 << 20) if last else VMEM,
    )[0]


def tokens_kernel(count, at_ref, own_in, other_in, gate_in, *refs):
    blocks, (own_out, other_out, own_w, other_w, gate_ref, tokens, sems) = refs[:count], refs[count:]
    loads = Loads(sems)
    head_dim, columns = own_w.shape
    mine = pl.ds(pl.multiple_of(at_ref[1] * columns, columns), columns)
    small = [
        loads.start(own_in.at[:, mine], own_w),
        loads.start(other_in, other_w),
        loads.start(gate_in.at[:, mine], gate_ref),
    ]
    parts = load_tokens(loads, blocks, tokens)
    for copy in small:
        copy.wait()
    total = None
    for here, copies in parts:
        weight = jnp.concatenate(
            [
                (ref[:, here].astype(jnp.float32) * gate_ref[:, here]).astype(jnp.bfloat16)
                for ref in (own_w, other_w)
            ],
            axis=0,
        )
        for copy in copies:
            copy.wait()
        part = dot(tokens[:, here], weight, 1, 1)
        total = part if total is None else total + part
    own_out[...] = total[:, :head_dim].astype(jnp.bfloat16)
    other_out[...] = total[:, head_dim:].astype(jnp.bfloat16)


def tokens_grad(at, own_w, other_w, gate, blocks):
    rows = sum(block.shape[0] for block in blocks)
    head_dim, columns = other_w.shape
    out = shape(rows, head_dim)
    return call(
        functools.partial(tokens_kernel, len(blocks)),
        "tokens_grad",
        10**8,
        [out, out],
        (at,),
        (own_w, other_w, gate, *blocks),
        [
            vmem(head_dim, columns),
            vmem(head_dim, columns),
            vmem(1, columns, dtype=jnp.float32),
            vmem(rows, columns),
            pltpu.SemaphoreType.DMA((3 + 2 * len(blocks),)),
        ],
    )


def sum_kernel(at_ref, pieces_ref, out_ref):
    count = pieces_ref.shape[0]
    total = pieces_ref[0].astype(jnp.float32)
    for index in range(1, count):
        total += pieces_ref[index].astype(jnp.float32)
    total = total.astype(jnp.bfloat16)
    y_hi = at_ref[1]
    for index in range(count):
        out_ref[y_hi * count + index] = total[:16]
        out_ref[(1 - y_hi) * count + index] = total[16:]


def sum_pieces(at, pieces):
    count, rows, columns = pieces.shape
    out = [shape(2 * count, rows // 2, columns)]
    return call(sum_kernel, "sum_pieces", 10**7, out, (at,), (pieces,), inner=True)[0]


def place_kernel(pieces_ref, out_ref):
    count, size, columns = pieces_ref.shape
    for index in range(count):
        half, piece = divmod(index, count // 2)
        rows = pl.ds(piece // 2 * size, size)
        here = pl.ds((half * 2 + piece % 2) * columns, columns)
        out_ref[rows, here] = pieces_ref[index].astype(jnp.float32)


def place_pieces(pieces):
    count, size, columns = pieces.shape
    out = [shape(count // 4 * size, 4 * columns, dtype=jnp.float32)]
    return call(place_kernel, "place_pieces", 10**7, out, (), (pieces,), inner=True)[0]


def after(array, *others):
    return lax.optimization_barrier((array, *others))[0]


def shards(queries, keys, values, cotangent, gate, w_out):
    query_head, key_head, value_head = queries[0, 0], keys[0, 0], values[0, 0]
    half = gate.shape[1] // 2
    seq = lax.axis_index("seq")
    y_hi = (seq // 2) % 2

    def columns(array, y):
        return lax.dynamic_slice_in_dim(array, y * half, half, 1)

    keep = columns(cotangent[0], y_hi)
    near, far, across = [send(keep, perm) for perm in (FROM_X1, FROM_X3, FROM_X2)]
    got = send(columns(cotangent[0], 1 - y_hi), SWAP_Y)
    w_other = send(columns(w_out, 1 - y_hi), MIRROR_Y)
    attn, inverse, weights = forward(query_head, key_head, value_head)
    at = jnp.stack([seq // 4, y_hi, seq % 2]).astype(jnp.int32)

    near, far, across, got, w_other, attn_on = lax.optimization_barrier((near, far, across, got, w_other, attn))
    early = [keep, near, across, far]
    swapped = [send(part, SWAP_CORE) for part in early]
    then = [got] + [send(got, perm) for perm in (FROM_X1, FROM_X2, FROM_X3)]
    attn_other = send(attn_on, SWAP_Y)

    def ends(y):
        return [(dx, e, y, 0, TOKENS) for dx in range(4) for e in range(2)]

    early = [part for pair in zip(early, swapped) for part in pair]
    own_1, other_1 = tokens_grad(at, w_out, w_other, gate, early)
    theirs_1 = send(other_1, SWAP_Y)
    partial = projection_grad(at, ends(0), after(attn, own_1), attn_other, early)
    then = lax.optimization_barrier((*then, partial, theirs_1))[:4]
    then = [part for block in then for part in (block, send(block, SWAP_CORE))]
    pieces = projection_grad(at, ends(1), attn, attn_other, then, gate, partial)
    own_2, other_2 = tokens_grad(at, after(w_out, pieces), w_other, gate, then)
    theirs_2 = send(other_2, SWAP_Y)
    pieces = lax.all_to_all(pieces, "hst", 0, 0, tiled=True)
    summed = sum_pieces(at, after(pieces, theirs_2))
    dq, dk, dv = backward(
        at,
        (ends(0), ends(1)),
        query_head,
        key_head,
        value_head,
        attn,
        inverse,
        weights,
        (after(own_1, summed), own_2),
        (theirs_1, theirs_2),
    )
    everywhere = lax.all_to_all(summed, AXES, 0, 0, tiled=True, axis_index_groups=FULL_Y)
    grad_out_proj = place_pieces(everywhere)
    return dq[None, None], dk[None, None], dv[None, None], grad_out_proj


def solution(mesh):
    in_specs = (
        P("hst", "seq", None, None),
        P("hst", "seq", None, None),
        P("hst", "seq", None, None),
        P("hst", "seq", None),
        P("hst", None),
        P("seq", None),
    )
    out_specs = (
        P("hst", "seq", None, None),
        P("hst", "seq", None, None),
        P("hst", "seq", None, None),
        P("seq", None),
    )
    return jax.shard_map(shards, mesh=mesh, in_specs=in_specs, out_specs=out_specs, check_vma=False)
```
